512 devices in a mesh: dp: 64 (over y, x, core), tensor: 8 (over z).
Axes of the slice: x: 4, y: 8, z: 8, core: 2. Of those that a mesh axis runs over, the one named last changes fastest.
Arguments:
- features: bfloat16 [16384, 3072], P('dp', 'tensor'), may hold values from -6 to 6
- out_grad: bfloat16 [16384, 1024], P('dp', 'tensor'), may hold values from -1.1953125 to 1.1953125
- weight: bfloat16 [3072, 1024], P('dp', 'tensor'), may hold values from -0.109375 to 0.109375
- feedback: float32 [196608, 1024], P('dp', 'tensor'), may hold values from -12 to 12
- warm_basis: float32 [1024, 32], P('tensor'), may hold values from -6 to 6
Outputs:
- input_grad: bfloat16 [16384, 3072], P('dp', 'tensor')
- new_feedback: float32 [196608, 1024], P('dp', 'tensor')
- new_basis: float32 [1024, 32], P('tensor')
The draws below stay inside these ranges and needn't reach their ends.
All inputs are finite; a program needn't handle non-finite values.
Results may differ from the reference program's by a relative error of at most 0.017.
Values may be sent and summed in bfloat16 or wider, within the bound.
No kernel may reach another device: no remote copies, remote signals or barrier semaphores. Data moves between devices by JAX's collectives and lax.ppermute only.
A program may use at most 64 MiB of HBM per device.

```python
import jax
import jax.numpy as jnp
from jax import lax

D_IN = 3072
HEAD_DIM = 128
HEADS_DEV = 1
RANK = 32
TOK_DEV = 256
TOKENS = 16384
COLUMNS = 1024
FB_ROWS = 196608
N_DP = 64
N_TENSOR = 8


def level_of(rng, dims, cuts, least, top_value):
    level = 1.0
    for axis_at, parts in cuts:
        draws = jax.random.uniform(jax.random.fold_in(jax.random.fold_in(rng, 6), axis_at), (parts,), jnp.float32, least / len(cuts), top_value / len(cuts))
        level = level * jnp.repeat(jnp.exp(draws), dims[axis_at] // parts).reshape((-1,) + (1,) * (len(dims) - 1 - axis_at))
    return level


def bell_draw(stream_key, dims, deviation, most, shards=(), dtype=jnp.bfloat16):
    entries = jax.random.normal(stream_key, dims, jnp.float32) * deviation
    if len(shards) > 0:
        entries = level_of(stream_key, dims, shards, -0.22, 0.18) * entries
    return jnp.clip(entries, min=-most, max=most).astype(dtype)


def setup_inputs(seed: int = 0) -> dict:
    keys = jax.random.split(jax.random.key(seed), 6)
    return {
        "features": bell_draw(keys[0], (TOKENS, D_IN), 1.0, 6.0, ((0, 64), (1, 8))),
        "out_grad": bell_draw(keys[1], (TOKENS, COLUMNS), 0.2, 1.1953125, ((0, 64), (1, 8))),
        "weight": bell_draw(keys[2], (D_IN, COLUMNS), D_IN ** -0.5, 0.109375, ((0, 64), (1, 8))),
        "feedback": bell_draw(keys[3], (FB_ROWS, COLUMNS), 2.0, 12.0, ((0, 64), (1, 8)), jnp.float32),
        "warm_basis": bell_draw(keys[4], (COLUMNS, RANK), 1.0, 6.0, ((0, 8),), jnp.float32),
    }


def reference(features, out_grad, weight, feedback, warm_basis):
    width = HEADS_DEV * HEAD_DIM
    highest = lax.Precision.HIGHEST
    inputs = features.astype(jnp.float32).reshape(N_DP, TOK_DEV, D_IN)
    grads_out = out_grad.reshape(N_DP, TOK_DEV, N_TENSOR, width).transpose(2, 0, 1, 3)
    states = feedback.reshape(N_DP, D_IN, N_TENSOR, width).transpose(2, 0, 1, 3)
    weights = weight.reshape(D_IN, N_TENSOR, width).transpose(1, 0, 2)
    bases = warm_basis.reshape(N_TENSOR, width, RANK)

    def per_block(total, operands):
        grad_block, state_block, weight_block, basis_block = operands
        grad_wide = grad_block.astype(jnp.float32)
        grads = jnp.einsum('rtd,rtc->rdc', inputs, grad_wide, precision=highest)
        merged = grads + state_block
        left = jnp.einsum('rdc,ck->dk', merged, basis_block, precision=highest) / N_DP
        gram_matrix = jnp.dot(left.T, left, precision=highest)
        factor = jnp.linalg.cholesky(gram_matrix)
        basis = jax.scipy.linalg.solve_triangular(factor, left.T, lower=True).T
        right = jnp.einsum('rdc,dk->ck', merged, basis, precision=highest) / N_DP
        approx = jnp.dot(basis, right.T, precision=highest)
        fresh = merged - approx[None]
        partial_value = jnp.einsum('rtc,dc->rtd', grad_wide, weight_block.astype(jnp.float32), precision=highest)
        total = total + partial_value.astype(jnp.bfloat16).astype(jnp.float32)
        return (total, (fresh, right))
    start_total = jnp.zeros((N_DP, TOK_DEV, D_IN), jnp.float32)
    total, outputs = lax.scan(per_block, start_total, (grads_out, states, weights, bases))
    fresh_all, rights = outputs
    new_feedback = fresh_all.transpose(1, 2, 0, 3).reshape(N_DP * D_IN, N_TENSOR * width)
    new_basis = rights.reshape(N_TENSOR * width, RANK)
    input_grad = total.reshape(N_DP * TOK_DEV, D_IN).astype(jnp.bfloat16)
    return (input_grad, new_feedback, new_basis)
```

```python
import jax
import jax.numpy as jnp
from jax import lax
from jax.experimental import pallas as pl
from jax.experimental.pallas import tpu as pltpu
from jax.sharding import Mesh, PartitionSpec as P

BF = jnp.bfloat16
F32 = jnp.float32
HIGHEST = lax.Precision.HIGHEST
CHIPS = ("y", "x")
DP = ("y", "x", "core")
N_Z = 8
N_CHIP = 32
REPLICAS = 64
D_IN = 3072
HALF = D_IN // 2
SLAB = D_IN // N_Z
PIECE = D_IN // REPLICAS
TOK = 256
COLS = 128
RANK = 32


def dot(a, b, dims, precision=None):
    return lax.dot_general(a, b, (dims, ((), ())), precision=precision, preferred_element_type=F32)


def partial_kernel(out_grad_ref, weight_ref, out_ref):
    for chip in range(4):
        for core in range(2):
            rows = weight_ref[core, chip]
            at = (chip * 2 + core) * PIECE
            out_ref[0, at : at + PIECE, :] = dot(rows, out_grad_ref[...], ((1,), (1,))).astype(BF)


def partial_call(out_grad, weight):
    return pl.pallas_call(
        partial_kernel,
        grid=(N_Z,),
        in_specs=[
            pl.BlockSpec((TOK, COLS), lambda z: (0, 0)),
            pl.BlockSpec((2, 4, PIECE, COLS), lambda z: (0, z, 0, 0)),
        ],
        out_specs=pl.BlockSpec((1, SLAB, TOK), lambda z: (z, 0, 0)),
        out_shape=jax.ShapeDtypeStruct((N_Z, SLAB, TOK), BF),
        cost_estimate=pl.CostEstimate(flops=2 * TOK * COLS * D_IN, bytes_accessed=2500000, transcendentals=0),
        name="partial_rows",
    )(out_grad, weight)


def merged_kernel(core_ref, features_ref, out_grad_ref, feedback_ref, merged_ref, send_ref, keep_ref):
    step = pl.program_id(0)
    merged = dot(features_ref[0], out_grad_ref[...], ((0,), (0,))) + feedback_ref[...]
    merged_ref[...] = merged

    @pl.when(step < N_Z // 2)
    def _():
        send_ref[...] = merged.astype(BF)

    @pl.when(step >= N_Z // 2)
    def _():
        keep_ref[...] = merged


def merged_call(core, features, out_grad, feedback):
    half = N_Z // 2

    def slab(step, core_ref):
        first = (1 - core_ref[0]) * half
        return lax.rem(first + step, N_Z)

    return pl.pallas_call(
        merged_kernel,
        grid_spec=pltpu.PrefetchScalarGridSpec(
            num_scalar_prefetch=1,
            grid=(N_Z,),
            in_specs=[
                pl.BlockSpec((1, TOK, SLAB), lambda s, c: (slab(s, c), 0, 0)),
                pl.BlockSpec((TOK, COLS), lambda s, c: (0, 0)),
                pl.BlockSpec((SLAB, COLS), lambda s, c: (slab(s, c), 0)),
            ],
            out_specs=[
                pl.BlockSpec((SLAB, COLS), lambda s, c: (slab(s, c), 0)),
                pl.BlockSpec((SLAB, COLS), lambda s, c: (jnp.minimum(s, half - 1), 0)),
                pl.BlockSpec((SLAB, COLS), lambda s, c: (jnp.maximum(s - half, 0), 0)),
            ],
        ),
        out_shape=[
            jax.ShapeDtypeStruct((D_IN, COLS), F32),
            jax.ShapeDtypeStruct((HALF, COLS), BF),
            jax.ShapeDtypeStruct((HALF, COLS), F32),
        ],
        cost_estimate=pl.CostEstimate(flops=2 * TOK * COLS * D_IN, bytes_accessed=6000000, transcendentals=0),
        name="merged_rows",
    )(core, features, out_grad, feedback)


def mean_kernel(parts_ref, out_ref):
    total = parts_ref[0].astype(F32)
    for chip in range(1, N_CHIP):
        total += parts_ref[chip].astype(F32)
    rounded = (total * (1.0 / REPLICAS)).astype(BF)
    for chip in range(N_CHIP):
        out_ref[chip] = rounded


def mean_call(parts):
    return pl.pallas_call(
        mean_kernel,
        out_shape=jax.ShapeDtypeStruct((N_CHIP, PIECE, COLS), BF),
        cost_estimate=pl.CostEstimate(flops=N_CHIP * PIECE * COLS, bytes_accessed=800000, transcendentals=0),
        name="mean_rows",
    )(parts)


def tail_kernel(mean_ref, merged_ref, warm_ref, fresh_ref, right_ref):
    mean = mean_ref[...]
    warm = warm_ref[...]
    outer = dot(mean, mean, ((0,), (0,)))
    right = dot(warm, outer, ((1,), (0,)), HIGHEST)
    gram = dot(right, warm, ((1,), (1,)), HIGHEST)
    row_at = lax.broadcasted_iota(jnp.int32, (RANK, 1), 0)
    for k in range(RANK):
        scale = lax.rsqrt(gram[k : k + 1, k : k + 1])
        column = jnp.where(row_at > k, gram[:, k : k + 1] * scale, 0.0)
        own = row_at == k
        gram_row = gram[k : k + 1] * scale
        right_row = right[k : k + 1] * scale
        warm_row = warm[k : k + 1] * scale
        gram = jnp.where(own, gram_row, gram - column * gram_row)
        right = jnp.where(own, right_row, right - column * right_row)
        warm = jnp.where(own, warm_row, warm - column * warm_row)
    right_ref[...] = right
    mix = dot(warm, right, ((0,), (0,)), HIGHEST)
    high = mix.astype(BF)
    low = (mix - high.astype(F32)).astype(BF)
    for slab in range(N_Z):
        rows = pl.ds(slab * SLAB, SLAB)
        block = mean_ref[rows, :]
        approx = dot(block, high, ((1,), (0,))) + dot(block, low, ((1,), (0,)))
        fresh_ref[rows, :] = merged_ref[rows, :] - approx


def tail_call(mean, merged, warm):
    return pl.pallas_call(
        tail_kernel,
        out_shape=[
            jax.ShapeDtypeStruct((D_IN, COLS), F32),
            jax.ShapeDtypeStruct((RANK, COLS), F32),
        ],
        cost_estimate=pl.CostEstimate(flops=6 * COLS * COLS * D_IN, bytes_accessed=4000000, transcendentals=32),
        name="basis_and_feedback",
    )(mean, merged, warm)


def to_all_chips(block):
    spread = lax.optimization_barrier(jnp.broadcast_to(block[None], (N_CHIP,) + block.shape))
    return lax.all_to_all(spread, CHIPS, 0, 0)


def on_device(features, out_grad, weight, feedback, warm_basis):
    core = lax.axis_index("core").astype(jnp.int32).reshape(1)
    gathered = lax.all_gather(features, "z", axis=0)
    weights = lax.all_gather(to_all_chips(weight), "core", axis=0)
    partial_rows = partial_call(out_grad, weights)
    input_grad = lax.psum_scatter(partial_rows, "z", scatter_dimension=0, tiled=False).T

    merged, send, keep = merged_call(core, gathered, out_grad, feedback)
    other = lax.ppermute(send, "core", [(0, 1), (1, 0)])
    chip_sum = (keep + other.astype(F32)).astype(BF).reshape(N_CHIP, PIECE, COLS)
    parts = lax.all_to_all(chip_sum, CHIPS, 0, 0)
    spread = mean_call(parts)
    half_mean = lax.all_to_all(spread, CHIPS, 0, 0).reshape(HALF, COLS)
    mean = lax.all_gather(half_mean, "core", axis=0, tiled=True)
    new_feedback, right = tail_call(mean, merged, warm_basis.T)
    return (input_grad, new_feedback, right.T)


def solution(mesh):
    grid = Mesh(mesh.devices.reshape(8, 4, 2, 8), ("y", "x", "core", "z"))
    return jax.shard_map(
        on_device,
        mesh=grid,
        in_specs=(P(DP, "z"), P(DP, "z"), P(DP, "z"), P(DP, "z"), P("z", None)),
        out_specs=(P(DP, "z"), P(DP, "z"), P("z", None)),
        check_vma=False,
    )
```

```python
import jax
import jax.numpy as jnp
from jax import lax
from jax.experimental import pallas as pl
from jax.experimental.pallas import tpu as pltpu
from jax.sharding import Mesh, PartitionSpec as P

BF = jnp.bfloat16
F32 = jnp.float32
HIGHEST = lax.Precision.HIGHEST
CHIPS = ("y", "x")
DP = ("y", "x", "core")
N_Z = 8
N_CHIP = 32
REPLICAS = 64
D_IN = 3072
HALF = D_IN // 2
SLAB = D_IN // N_Z
PIECE = D_IN // REPLICAS
TOK = 256
COLS = 128
RANK = 32


def dot(a, b, dims, precision=None):
    return lax.dot_general(a, b, (dims, ((), ())), precision=precision, preferred_element_type=F32)


def partial_kernel(out_grad_ref, weight_ref, out_ref):
    rows = [weight_ref[core, chip] for chip in range(4) for core in range(2)]
    slab = jnp.concatenate(rows, axis=0)
    out_ref[0] = dot(out_grad_ref[...], slab, ((1,), (1,))).astype(BF)


def partial_call(out_grad, weight):
    return pl.pallas_call(
        partial_kernel,
        grid=(N_Z,),
        in_specs=[
            pl.BlockSpec((TOK, COLS), lambda z: (0, 0)),
            pl.BlockSpec((2, 4, PIECE, COLS), lambda z: (0, z, 0, 0)),
        ],
        out_specs=pl.BlockSpec((1, TOK, SLAB), lambda z: (z, 0, 0)),
        out_shape=jax.ShapeDtypeStruct((N_Z, TOK, SLAB), BF),
        cost_estimate=pl.CostEstimate(flops=2 * TOK * COLS * D_IN, bytes_accessed=2500000, transcendentals=0),
        name="partial_slabs",
    )(out_grad, weight)


def tail_kernel(mean_ref, merged_ref, warm_ref, fresh_ref, right_ref, merged_buf, fresh_buf, in_sems, out_sems):
    bands = merged_buf.shape[0]
    band = D_IN // bands
    loads = [
        pltpu.make_async_copy(merged_ref.at[pl.ds(i * band, band)], merged_buf.at[i], in_sems.at[i])
        for i in range(bands)
    ]
    stores = [
        pltpu.make_async_copy(fresh_buf.at[i], fresh_ref.at[pl.ds(i * band, band)], out_sems.at[i])
        for i in range(bands)
    ]
    for load in loads:
        load.start()
    mean = mean_ref[...]
    warm = warm_ref[...]
    outer = dot(mean, mean, ((0,), (0,)))
    right = dot(warm, outer, ((1,), (0,)), HIGHEST)
    gram = dot(right, warm, ((1,), (1,)), HIGHEST)
    row_at = lax.broadcasted_iota(jnp.int32, (RANK, 1), 0)
    for k in range(RANK):
        scale = lax.rsqrt(gram[k : k + 1, k : k + 1])
        column = jnp.where(row_at > k, gram[:, k : k + 1] * scale, 0.0)
        own = row_at == k
        gram_row = gram[k : k + 1] * scale
        right_row = right[k : k + 1] * scale
        warm_row = warm[k : k + 1] * scale
        gram = jnp.where(own, gram_row, gram - column * gram_row)
        right = jnp.where(own, right_row, right - column * right_row)
        warm = jnp.where(own, warm_row, warm - column * warm_row)
    right_ref[...] = right
    mix = dot(warm, right, ((0,), (0,)), HIGHEST)
    high = mix.astype(BF)
    low = (mix - high.astype(F32)).astype(BF)
    for i in range(bands):
        block = mean_ref[i * band : (i + 1) * band, :]
        approx = dot(block, high, ((1,), (0,))) + dot(block, low, ((1,), (0,)))
        loads[i].wait()
        fresh_buf[i] = merged_buf[i] - approx
        stores[i].start()
    for store in stores:
        store.wait()


def tail_call(mean, merged, warm):
    bands = 4
    in_vmem = pl.BlockSpec(memory_space=pltpu.VMEM)
    in_hbm = pl.BlockSpec(memory_space=pl.ANY)
    return pl.pallas_call(
        tail_kernel,
        in_specs=[in_vmem, in_hbm, in_vmem],
        out_specs=[in_hbm, in_vmem],
        out_shape=[
            jax.ShapeDtypeStruct((D_IN, COLS), F32),
            jax.ShapeDtypeStruct((RANK, COLS), F32),
        ],
        scratch_shapes=[
            pltpu.VMEM((bands, D_IN // bands, COLS), F32),
            pltpu.VMEM((bands, D_IN // bands, COLS), F32),
            pltpu.SemaphoreType.DMA((bands,)),
            pltpu.SemaphoreType.DMA((bands,)),
        ],
        cost_estimate=pl.CostEstimate(flops=6 * COLS * COLS * D_IN, bytes_accessed=4000000, transcendentals=32),
        name="basis_and_feedback",
    )(mean, merged, warm)


def to_all_chips(block):
    spread = lax.optimization_barrier(jnp.broadcast_to(block[None], (N_CHIP,) + block.shape))
    return lax.all_to_all(spread, CHIPS, 0, 0)


def swap_cores(block):
    return lax.ppermute(block, "core", [(0, 1), (1, 0)])


def on_device(features, out_grad, weight, feedback, warm_basis):
    core = lax.axis_index("core")
    gathered = lax.all_gather(features, ("core", "z"), axis=0).reshape(2, N_Z, TOK, SLAB)

    weights = lax.all_gather(to_all_chips(weight), "core", axis=0)
    partial_slabs = partial_call(out_grad, weights)
    pair_out_grad = lax.all_gather(out_grad, "core", axis=0)
    other_half = swap_cores(lax.dynamic_slice_in_dim(feedback, (1 - core) * HALF, HALF))
    own_half = lax.dynamic_slice_in_dim(feedback, core * HALF, HALF)
    chip_feedback = lax.optimization_barrier(own_half + other_half)
    input_grad = lax.psum_scatter(partial_slabs, "z", scatter_dimension=0, tiled=False)

    half_features = lax.dynamic_slice_in_dim(gathered, core * (N_Z // 2), N_Z // 2, axis=1)
    chip_grad = jnp.einsum("szta,stb->zab", half_features, pair_out_grad, preferred_element_type=F32)
    chip_sum = (chip_grad.reshape(HALF, COLS) + chip_feedback).astype(BF)
    parts = lax.all_to_all(chip_sum.reshape(N_CHIP, PIECE, COLS), CHIPS, 0, 0)

    own_features = lax.dynamic_index_in_dim(gathered, core, 0, keepdims=False)
    grad = jnp.einsum("zta,tb->zab", own_features, out_grad, preferred_element_type=F32)
    merged = grad.reshape(D_IN, COLS) + feedback

    piece = (jnp.sum(parts.astype(F32), axis=0) / REPLICAS).astype(BF)
    half_mean = to_all_chips(piece).reshape(HALF, COLS)
    mean = lax.all_gather(half_mean, "core", axis=0, tiled=True)
    new_feedback, right = tail_call(mean, merged, warm_basis.T)
    return (input_grad, new_feedback, right.T)


def solution(mesh):
    grid = Mesh(mesh.devices.reshape(8, 4, 2, 8), ("y", "x", "core", "z"))
    return jax.shard_map(
        on_device,
        mesh=grid,
        in_specs=(P(DP, "z"), P(DP, "z"), P(DP, "z"), P(DP, "z"), P("z", None)),
        out_specs=(P(DP, "z"), P(DP, "z"), P("z", None)),
        check_vma=False,
    )
```

```python
import jax
import jax.numpy as jnp
from jax import lax
from jax.experimental import pallas as pl
from jax.experimental.pallas import tpu as pltpu
from jax.sharding import Mesh, PartitionSpec as P

BF = jnp.bfloat16
F32 = jnp.float32
HIGHEST = lax.Precision.HIGHEST
CHIPS = ("y", "x")
DP = ("y", "x", "core")
TENSOR = ("zh", "zl")
N_ZL = 4
N_CHIP = 32
REPLICAS = 64
D_IN = 3072
HALF = D_IN // 2
QUARTER = D_IN // 4
SLAB = D_IN // 8
PIECE = D_IN // REPLICAS
TOK = 256
COLS = 128
RANK = 32


def dot(a, b, dims, precision=None):
    return lax.dot_general(a, b, (dims, ((), ())), precision=precision, preferred_element_type=F32)


def tail_kernel(
    place_ref, mean_ref, own_ref, other_ref, warm_ref, pairs_ref, weight_ref,
    fresh_ref, right_ref, input_grad_ref,
    own_buf, other_buf, fresh_buf, pairs_buf, weight_buf, sems, out_sems,
):
    zh = place_ref[0]
    loads = [
        pltpu.make_async_copy(pairs_ref, pairs_buf, sems.at[0]),
        pltpu.make_async_copy(weight_ref, weight_buf, sems.at[1]),
        pltpu.make_async_copy(own_ref, own_buf, sems.at[2]),
        pltpu.make_async_copy(other_ref, other_buf, sems.at[3]),
    ]
    for load in loads:
        load.start()
    mean = mean_ref[...]
    warm = warm_ref[...]
    outer = dot(mean, mean, ((0,), (0,)))
    right = dot(warm, outer, ((1,), (0,)), HIGHEST)
    gram = dot(right, warm, ((1,), (1,)), HIGHEST)

    loads[0].wait()
    loads[1].wait()
    total = jnp.zeros((TOK, SLAB), F32)
    for half in range(2):
        start = pl.multiple_of((zh if half == 0 else 1 - zh) * COLS, COLS)
        for zl in range(N_ZL):
            grads = pairs_buf[zl, :, pl.ds(start, COLS)]
            block = (half * N_ZL + zl) * 4
            rows = [weight_buf[core, block + x] for x in range(4) for core in range(2)]
            total += dot(grads, jnp.concatenate(rows, axis=0), ((1,), (1,)))
    input_grad_ref[...] = total.astype(BF)

    row_at = lax.broadcasted_iota(jnp.int32, (RANK, 1), 0)
    for k in range(RANK):
        scale = lax.rsqrt(gram[k : k + 1, k : k + 1])
        column = jnp.where(row_at > k, gram[:, k : k + 1] * scale, 0.0)
        own = row_at == k
        gram_row = gram[k : k + 1] * scale
        right_row = right[k : k + 1] * scale
        warm_row = warm[k : k + 1] * scale
        gram = jnp.where(own, gram_row, gram - column * gram_row)
        right = jnp.where(own, right_row, right - column * right_row)
        warm = jnp.where(own, warm_row, warm - column * warm_row)
    right_ref[...] = right
    mix = dot(warm, right, ((0,), (0,)), HIGHEST)
    high = mix.astype(BF)
    low = (mix - high.astype(F32)).astype(BF)

    for load in loads[2:]:
        load.wait()
    stores = []
    for core in range(2):
        for side in range(2):
            at = core * 2 + side
            block = mean_ref[at * QUARTER : (at + 1) * QUARTER, :]
            approx = dot(block, high, ((1,), (0,))) + dot(block, low, ((1,), (0,)))
            merged = (own_buf, other_buf)[side][core * QUARTER : (core + 1) * QUARTER]
            fresh_buf[at] = merged - approx
            half = zh if side == 0 else 1 - zh
            start = pl.multiple_of(half * HALF + core * QUARTER, QUARTER)
            store = pltpu.make_async_copy(fresh_buf.at[at], fresh_ref.at[pl.ds(start, QUARTER)], out_sems.at[at])
            store.start()
            stores.append(store)
    for store in stores:
        store.wait()


def tail_call(place, mean, own_merged, other_merged, warm, pairs, weights):
    in_vmem = pl.BlockSpec(memory_space=pltpu.VMEM)
    in_hbm = pl.BlockSpec(memory_space=pl.ANY)
    return pl.pallas_call(
        tail_kernel,
        in_specs=[pl.BlockSpec(memory_space=pltpu.SMEM), in_vmem, in_hbm, in_hbm, in_vmem, in_hbm, in_hbm],
        out_specs=[in_hbm, in_vmem, in_vmem],
        out_shape=[
            jax.ShapeDtypeStruct((D_IN, COLS), F32),
            jax.ShapeDtypeStruct((RANK, COLS), F32),
            jax.ShapeDtypeStruct((TOK, SLAB), BF),
        ],
        scratch_shapes=[
            pltpu.VMEM((HALF, COLS), F32),
            pltpu.VMEM((HALF, COLS), F32),
            pltpu.VMEM((4, QUARTER, COLS), F32),
            pltpu.VMEM((N_ZL, TOK, 2 * COLS), BF),
            pltpu.VMEM((2, N_CHIP, PIECE, COLS), BF),
            pltpu.SemaphoreType.DMA((4,)),
            pltpu.SemaphoreType.DMA((4,)),
        ],
        compiler_params=pltpu.CompilerParams(vmem_limit_bytes=32 * 1024 * 1024),
        cost_estimate=pl.CostEstimate(flops=8 * COLS * COLS * D_IN, bytes_accessed=5000000, transcendentals=32),
        name="basis_feedback_input_grad",
    )(place, mean, own_merged, other_merged, warm, pairs, weights)


def swap_cores(block):
    return lax.ppermute(block, "core", [(0, 1), (1, 0)])


def swap_halves(block):
    return lax.ppermute(block, "zh", [(0, 1), (1, 0)])


def pick(block, at):
    return lax.dynamic_index_in_dim(block, at, 0, keepdims=False)


def to_all_chips(block):
    spread = lax.optimization_barrier(jnp.broadcast_to(block[None], (N_CHIP,) + block.shape))
    return lax.all_to_all(spread, CHIPS, 0, 0)


def on_device(features, out_grad, weight, feedback, warm_basis):
    core = lax.axis_index("core")
    zh = lax.axis_index("zh")
    barrier = lax.optimization_barrier

    partner_out_grad = swap_halves(out_grad)
    plane = [(i * 8 + j, j * 8 + i) for i in range(8) for j in range(8)]
    turned = lax.ppermute(weight, ("y",) + TENSOR, plane)

    gathered = lax.all_gather(features, "zl", axis=1, tiled=True)
    gathered, turned = barrier((gathered, turned))
    sent = dot(gathered, partner_out_grad, ((0,), (0,))).astype(BF)
    other_grads = swap_halves(sent)
    chip_weights = to_all_chips(turned)
    by_half = feedback.reshape(2, HALF, COLS)
    own_merged = dot(gathered, out_grad, ((0,), (0,))) + pick(by_half, zh)

    def chip_sum(rows):
        quarters = rows.reshape(2, QUARTER, COLS)
        other = swap_cores(pick(quarters, 1 - core).astype(BF))
        return (pick(quarters, core) + other.astype(F32)).astype(BF)

    own_sum = chip_sum(own_merged)
    other_merged = other_grads.astype(F32) + pick(by_half, 1 - zh)
    other_sum = chip_sum(other_merged)
    chips = jnp.concatenate([own_sum, other_sum], axis=0).reshape(N_CHIP, PIECE, COLS)

    chips, chip_weights, own_late, partner_late = barrier((chips, chip_weights, out_grad, partner_out_grad))
    parts = lax.all_to_all(chips, CHIPS, 0, 0)
    pairs = lax.all_gather(jnp.concatenate([own_late, partner_late], axis=1), "zl", axis=0)
    parts, pairs = barrier((parts, pairs))

    piece = (jnp.sum(parts.astype(F32), axis=0) / REPLICAS).astype(BF)
    piece, chip_weights = barrier((piece, chip_weights))
    weights = lax.all_gather(chip_weights, "core", axis=0)
    all_means = lax.all_gather(to_all_chips(piece), "core", axis=0).reshape(D_IN, COLS)
    place = zh.astype(jnp.int32).reshape(1)
    new_feedback, right, input_grad = tail_call(
        place, all_means, own_merged, other_merged, warm_basis.T, pairs, weights
    )
    return (input_grad, new_feedback, right.T)


def solution(mesh):
    grid = Mesh(mesh.devices.reshape(8, 4, 2, 2, 4), DP + TENSOR)
    return jax.shard_map(
        on_device,
        mesh=grid,
        in_specs=(P(DP, TENSOR), P(DP, TENSOR), P(DP, TENSOR), P(DP, TENSOR), P(TENSOR, None)),
        out_specs=(P(DP, TENSOR), P(DP, TENSOR), P(TENSOR, None)),
        check_vma=False,
    )
```

```python
import jax
import jax.numpy as jnp
from jax import lax
from jax.experimental import pallas as pl
from jax.experimental.pallas import tpu as pltpu
from jax.sharding import Mesh, PartitionSpec as P

BF = jnp.bfloat16
F32 = jnp.float32
HIGHEST = lax.Precision.HIGHEST
CHIPS = ("y", "x")
DP = ("y", "x", "core")
TENSOR = ("zl", "zh")
N_ZL = 4
N_CHIP = 32
REPLICAS = 64
D_IN = 3072
HALF = D_IN // 2
QUARTER = D_IN // 4
SLAB = D_IN // 8
PIECE = D_IN // REPLICAS
TOK = 256
COLS = 128
RANK = 32


def dot(a, b, dims, precision=None):
    return lax.dot_general(a, b, (dims, ((), ())), precision=precision, preferred_element_type=F32)


def tail_kernel(
    place_ref, mean_ref, own_ref, other_ref, warm_ref, near_ref, far_ref, weight_ref,
    fresh_ref, right_ref, input_grad_ref,
    own_buf, other_buf, fresh_buf, out_grad_buf, weight_buf, sems, out_sems,
):
    zh = place_ref[0]
    loads = [
        pltpu.make_async_copy(near_ref, out_grad_buf.at[0], sems.at[0]),
        pltpu.make_async_copy(far_ref, out_grad_buf.at[1], sems.at[1]),
        pltpu.make_async_copy(weight_ref, weight_buf, sems.at[2]),
        pltpu.make_async_copy(own_ref, own_buf, sems.at[3]),
        pltpu.make_async_copy(other_ref, other_buf, sems.at[4]),
    ]
    for load in loads:
        load.start()
    mean = mean_ref[...]
    warm = warm_ref[...]
    outer = dot(mean, mean, ((0,), (0,)))
    right = dot(warm, outer, ((1,), (0,)), HIGHEST)
    gram = dot(right, warm, ((1,), (1,)), HIGHEST)

    for load in loads[:3]:
        load.wait()
    total = jnp.zeros((TOK, SLAB), F32)
    for half in range(2):
        side = zh if half == 0 else 1 - zh
        for zl in range(N_ZL):
            grads = out_grad_buf[side, zl]
            block = (zl * 2 + half) * 4
            rows = [weight_buf[core, block + x] for x in range(4) for core in range(2)]
            total += dot(grads, jnp.concatenate(rows, axis=0), ((1,), (1,)))
    input_grad_ref[...] = total.astype(BF)

    row_at = lax.broadcasted_iota(jnp.int32, (RANK, 1), 0)
    for k in range(RANK):
        scale = lax.rsqrt(gram[k : k + 1, k : k + 1])
        column = jnp.where(row_at > k, gram[:, k : k + 1] * scale, 0.0)
        own = row_at == k
        gram_row = gram[k : k + 1] * scale
        right_row = right[k : k + 1] * scale
        warm_row = warm[k : k + 1] * scale
        gram = jnp.where(own, gram_row, gram - column * gram_row)
        right = jnp.where(own, right_row, right - column * right_row)
        warm = jnp.where(own, warm_row, warm - column * warm_row)
    right_ref[...] = right
    mix = dot(warm, right, ((0,), (0,)), HIGHEST)
    high = mix.astype(BF)
    low = (mix - high.astype(F32)).astype(BF)

    for load in loads[3:]:
        load.wait()
    stores = []
    for core in range(2):
        for side in range(2):
            at = core * 2 + side
            block = mean_ref[at * QUARTER : (at + 1) * QUARTER, :]
            approx = dot(block, high, ((1,), (0,))) + dot(block, low, ((1,), (0,)))
            merged = (own_buf, other_buf)[side][core * QUARTER : (core + 1) * QUARTER]
            fresh_buf[at] = merged - approx
            half = zh if side == 0 else 1 - zh
            for slab in range(2):
                start = pl.multiple_of(((core * 2 + slab) * 2 + half) * SLAB, SLAB)
                store = pltpu.make_async_copy(
                    fresh_buf.at[at, pl.ds(slab * SLAB, SLAB)],
                    fresh_ref.at[pl.ds(start, SLAB)],
                    out_sems.at[at, slab],
                )
                store.start()
                stores.append(store)
    for store in stores:
        store.wait()


def tail_call(place, mean, own_merged, other_merged, warm, near, far, weights):
    in_vmem = pl.BlockSpec(memory_space=pltpu.VMEM)
    in_hbm = pl.BlockSpec(memory_space=pl.ANY)
    return pl.pallas_call(
        tail_kernel,
        in_specs=[pl.BlockSpec(memory_space=pltpu.SMEM), in_vmem, in_hbm, in_hbm, in_vmem] + [in_hbm] * 3,
        out_specs=[in_hbm, in_vmem, in_vmem],
        out_shape=[
            jax.ShapeDtypeStruct((D_IN, COLS), F32),
            jax.ShapeDtypeStruct((RANK, COLS), F32),
            jax.ShapeDtypeStruct((TOK, SLAB), BF),
        ],
        scratch_shapes=[
            pltpu.VMEM((HALF, COLS), F32),
            pltpu.VMEM((HALF, COLS), F32),
            pltpu.VMEM((4, QUARTER, COLS), F32),
            pltpu.VMEM((2, N_ZL, TOK, COLS), BF),
            pltpu.VMEM((2, N_CHIP, PIECE, COLS), BF),
            pltpu.SemaphoreType.DMA((5,)),
            pltpu.SemaphoreType.DMA((4, 2)),
        ],
        compiler_params=pltpu.CompilerParams(vmem_limit_bytes=32 * 1024 * 1024),
        cost_estimate=pl.CostEstimate(flops=8 * COLS * COLS * D_IN, bytes_accessed=5000000, transcendentals=32),
        name="basis_feedback_input_grad",
    )(place, mean, own_merged, other_merged, warm, near, far, weights)


def swap_halves(block):
    return lax.ppermute(block, "zh", [(0, 1), (1, 0)])


def pick(block, at):
    return lax.dynamic_index_in_dim(block, at, 0, keepdims=False)


def to_all_chips(block):
    spread = lax.optimization_barrier(jnp.broadcast_to(block[None], (N_CHIP,) + block.shape))
    return lax.all_to_all(spread, CHIPS, 0, 0)


def on_device(features, out_grad, weight, feedback, warm_basis):
    core = lax.axis_index("core")
    zh = lax.axis_index("zh")
    barrier = lax.optimization_barrier

    partner_out_grad = swap_halves(out_grad)
    plane = [(i * 8 + j, j * 8 + i) for i in range(8) for j in range(8)]
    turned = lax.ppermute(weight, ("y",) + TENSOR, plane)

    gathered = lax.all_gather(features, "zl", axis=1, tiled=True)
    gathered, turned = barrier((gathered, turned))
    sent = dot(gathered, partner_out_grad, ((0,), (0,))).astype(BF)
    other_grads = swap_halves(sent)
    chip_weights = to_all_chips(turned)
    slabs = feedback.reshape(N_ZL, 2, SLAB, COLS)

    def add_feedback(grads, half):
        own = lax.dynamic_slice(slabs, (0, half, 0, 0), (N_ZL, 1, SLAB, COLS))
        return (grads.reshape(own.shape).astype(F32) + own).reshape(HALF, COLS)

    own_merged = add_feedback(dot(gathered, out_grad, ((0,), (0,))), zh)

    other_merged = add_feedback(other_grads, 1 - zh)

    def quarters(at):
        return jnp.stack([pick(rows.reshape(2, QUARTER, COLS), at) for rows in (own_merged, other_merged)])

    swapped = lax.all_gather(quarters(1 - core).astype(BF), "core", axis=0)
    chips = (quarters(core) + pick(swapped, 1 - core).astype(F32)).astype(BF).reshape(N_CHIP, PIECE, COLS)

    chips, chip_weights, late = barrier((chips, chip_weights, out_grad))
    parts = lax.all_to_all(chips, CHIPS, 0, 0)
    near = lax.all_gather(late, "zl", axis=0)
    parts, near = barrier((parts, near))

    piece = (jnp.sum(parts.astype(F32), axis=0) / REPLICAS).astype(BF)
    piece, chip_weights, near = barrier((piece, chip_weights, near))
    far = swap_halves(near)
    weights = lax.all_gather(chip_weights, "core", axis=0)
    all_means = lax.all_gather(to_all_chips(piece), "core", axis=0).reshape(D_IN, COLS)
    place = zh.astype(jnp.int32).reshape(1)
    new_feedback, right, input_grad = tail_call(
        place, all_means, own_merged, other_merged, warm_basis.T, near, far, weights
    )
    return (input_grad, new_feedback, right.T)


def solution(mesh):
    grid = Mesh(mesh.devices.reshape(8, 4, 2, 4, 2), DP + TENSOR)
    return jax.shard_map(
        on_device,
        mesh=grid,
        in_specs=(P(DP, TENSOR), P(DP, TENSOR), P(DP, TENSOR), P(DP, TENSOR), P(TENSOR, None)),
        out_specs=(P(DP, TENSOR), P(DP, TENSOR), P(TENSOR, None)),
        check_vma=False,
    )
```

```python
import jax
import jax.numpy as jnp
from jax import lax
from jax.experimental import pallas as pl
from jax.experimental.pallas import tpu as pltpu
from jax.sharding import Mesh, PartitionSpec as P

BF = jnp.bfloat16
F32 = jnp.float32
HIGHEST = lax.Precision.HIGHEST
CHIPS = ("y", "x")
DP = ("y", "x", "core")
TENSOR = ("zl", "zh")
N_ZL = 4
N_CHIP = 32
REPLICAS = 64
D_IN = 3072
HALF = D_IN // 2
QUARTER = D_IN // 4
SLAB = D_IN // 8
PIECE = D_IN // REPLICAS
TOK = 256
COLS = 128
RANK = 32
EARLY = 32


def dot(a, b, dims, precision=None):
    return lax.dot_general(a, b, (dims, ((), ())), precision=precision, preferred_element_type=F32)


def tail_kernel(
    place_ref, mean_ref, own_ref, other_ref, warm_ref, near_ref, far_ref, weight_ref,
    fresh_ref, right_ref, input_grad_ref,
    own_buf, other_buf, fresh_buf, out_grad_buf, weight_buf, sems, out_sems,
):
    zh, zl = place_ref[0], place_ref[1]
    loads = [
        pltpu.make_async_copy(near_ref, out_grad_buf.at[0], sems.at[0]),
        pltpu.make_async_copy(far_ref, out_grad_buf.at[1], sems.at[1]),
        pltpu.make_async_copy(weight_ref, weight_buf, sems.at[2]),
        pltpu.make_async_copy(own_ref, own_buf, sems.at[3]),
        pltpu.make_async_copy(other_ref, other_buf, sems.at[4]),
    ]
    for load in loads:
        load.start()
    mean = mean_ref[...]
    warm = warm_ref[...]
    outer = dot(mean, mean, ((0,), (0,)))
    right = dot(warm, outer, ((1,), (0,)), HIGHEST)
    gram = dot(right, warm, ((1,), (1,)), HIGHEST)

    for load in loads[:3]:
        load.wait()
    total = jnp.zeros((TOK, SLAB), F32)
    for half in range(2):
        side = zh if half == 0 else 1 - zh
        for at in range(N_ZL):
            grads = out_grad_buf[side, at]
            block = (at * 2 + half) * 4
            rows = [weight_buf[core, block + x] for x in range(4) for core in range(2)]
            total += dot(grads, jnp.concatenate(rows, axis=0), ((1,), (1,)))
    input_grad_ref[...] = total.astype(BF)

    row_at = lax.broadcasted_iota(jnp.int32, (RANK, 1), 0)
    for k in range(RANK):
        scale = lax.rsqrt(gram[k : k + 1, k : k + 1])
        column = jnp.where(row_at > k, gram[:, k : k + 1] * scale, 0.0)
        own = row_at == k
        gram_row = gram[k : k + 1] * scale
        right_row = right[k : k + 1] * scale
        warm_row = warm[k : k + 1] * scale
        gram = jnp.where(own, gram_row, gram - column * gram_row)
        right = jnp.where(own, right_row, right - column * right_row)
        warm = jnp.where(own, warm_row, warm - column * warm_row)
    right_ref[...] = right
    mix = dot(warm, right, ((0,), (0,)), HIGHEST)
    high = mix.astype(BF)
    low = (mix - high.astype(F32)).astype(BF)

    for load in loads[3:]:
        load.wait()
    stores = []
    for core in range(2):
        for side in range(2):
            at = core * 2 + side
            block = mean_ref[at * QUARTER : (at + 1) * QUARTER, :]
            approx = dot(block, high, ((1,), (0,))) + dot(block, low, ((1,), (0,)))
            merged = (own_buf, other_buf)[side][core * QUARTER : (core + 1) * QUARTER]
            fresh_buf[at] = merged - approx
            half = zh if side == 0 else 1 - zh
            for slab in range(2):
                owner = (zl + N_ZL - (core * 2 + slab)) % N_ZL
                start = pl.multiple_of((owner * 2 + half) * SLAB, SLAB)
                store = pltpu.make_async_copy(
                    fresh_buf.at[at, pl.ds(slab * SLAB, SLAB)],
                    fresh_ref.at[pl.ds(start, SLAB)],
                    out_sems.at[at, slab],
                )
                store.start()
                stores.append(store)
    for store in stores:
        store.wait()


def tail_call(place, mean, own_merged, other_merged, warm, near, far, weights):
    in_vmem = pl.BlockSpec(memory_space=pltpu.VMEM)
    in_hbm = pl.BlockSpec(memory_space=pl.ANY)
    return pl.pallas_call(
        tail_kernel,
        in_specs=[pl.BlockSpec(memory_space=pltpu.SMEM), in_vmem, in_hbm, in_hbm, in_vmem] + [in_hbm] * 3,
        out_specs=[in_hbm, in_vmem, in_vmem],
        out_shape=[
            jax.ShapeDtypeStruct((D_IN, COLS), F32),
            jax.ShapeDtypeStruct((RANK, COLS), F32),
            jax.ShapeDtypeStruct((TOK, SLAB), BF),
        ],
        scratch_shapes=[
            pltpu.VMEM((HALF, COLS), F32),
            pltpu.VMEM((HALF, COLS), F32),
            pltpu.VMEM((4, QUARTER, COLS), F32),
            pltpu.VMEM((2, N_ZL, TOK, COLS), BF),
            pltpu.VMEM((2, N_CHIP, PIECE, COLS), BF),
            pltpu.SemaphoreType.DMA((5,)),
            pltpu.SemaphoreType.DMA((4, 2)),
        ],
        compiler_params=pltpu.CompilerParams(vmem_limit_bytes=32 * 1024 * 1024),
        cost_estimate=pl.CostEstimate(flops=8 * COLS * COLS * D_IN, bytes_accessed=5000000, transcendentals=32),
        name="basis_feedback_input_grad",
    )(place, mean, own_merged, other_merged, warm, near, far, weights)


def swap_halves(block):
    return lax.ppermute(block, "zh", [(0, 1), (1, 0)])


def pick(block, at):
    return lax.dynamic_index_in_dim(block, at, 0, keepdims=False)


def to_all_chips(block):
    spread = lax.optimization_barrier(jnp.broadcast_to(block[None], (N_CHIP,) + block.shape))
    return lax.all_to_all(spread, CHIPS, 0, 0)


def on_device(features, out_grad, weight, feedback, warm_basis):
    core = lax.axis_index("core")
    zh = lax.axis_index("zh")
    zl = lax.axis_index("zl")
    barrier = lax.optimization_barrier

    partner_out_grad = swap_halves(out_grad)
    plane = [(i * 8 + j, j * 8 + i) for i in range(8) for j in range(8)]
    turned = lax.ppermute(weight, ("y",) + TENSOR, plane)

    shifted = [features] + [
        lax.ppermute(features, "zl", [(i, (i + k) % N_ZL) for i in range(N_ZL)]) for k in range(1, N_ZL)
    ]
    spread = jnp.broadcast_to(turned[None, :EARLY], (N_CHIP, EARLY, COLS))
    shifted, spread = barrier((shifted, spread))
    gathered = jnp.concatenate(shifted, axis=1)
    sent = dot(gathered, partner_out_grad, ((0,), (0,))).astype(BF)
    other_grads = swap_halves(sent)
    early_weights = lax.all_to_all(spread, CHIPS, 0, 0)
    natural = feedback.reshape(N_ZL, 2, SLAB, COLS)
    slabs = [lax.dynamic_slice_in_dim(natural, (zl + N_ZL - k) % N_ZL, 1) for k in range(N_ZL)]
    slabs = barrier(jnp.concatenate(slabs, axis=0))

    def add_feedback(grads, half):
        own = lax.dynamic_slice(slabs, (0, half, 0, 0), (N_ZL, 1, SLAB, COLS))
        return (grads.reshape(own.shape).astype(F32) + own).reshape(HALF, COLS)

    own_merged = add_feedback(dot(gathered, out_grad, ((0,), (0,))), zh)

    other_merged = add_feedback(other_grads, 1 - zh)

    def quarters(at):
        return jnp.stack([pick(rows.reshape(2, QUARTER, COLS), at) for rows in (own_merged, other_merged)])

    swapped = lax.all_gather(quarters(1 - core).astype(BF), "core", axis=0)
    chips = (quarters(core) + pick(swapped, 1 - core).astype(F32)).astype(BF).reshape(N_CHIP, PIECE, COLS)

    late_weight = jnp.broadcast_to(turned[None, EARLY:], (N_CHIP, PIECE - EARLY, COLS))
    load = jnp.concatenate([chips, late_weight], axis=1)
    load, early_weights, late = barrier((load, early_weights, out_grad))
    arrived = lax.all_to_all(load, CHIPS, 0, 0)
    near = lax.all_gather(late, "zl", axis=0)
    arrived, near = barrier((arrived, near))
    parts = arrived[:, :PIECE]

    piece = (jnp.sum(parts.astype(F32), axis=0) / REPLICAS).astype(BF)
    piece, early_weights, arrived, near = barrier((piece, early_weights, arrived, near))
    chip_weights = jnp.concatenate([early_weights, arrived[:, PIECE:]], axis=1)
    far = swap_halves(near)
    weights = lax.all_gather(chip_weights, "core", axis=0)
    all_means = lax.all_gather(to_all_chips(piece), "core", axis=0).reshape(D_IN, COLS)
    place = jnp.stack([zh, zl]).astype(jnp.int32)
    new_feedback, right, input_grad = tail_call(
        place, all_means, own_merged, other_merged, warm_basis.T, near, far, weights
    )
    return (input_grad, new_feedback, right.T)


def solution(mesh):
    grid = Mesh(mesh.devices.reshape(8, 4, 2, 4, 2), DP + TENSOR)
    return jax.shard_map(
        on_device,
        mesh=grid,
        in_specs=(P(DP, TENSOR), P(DP, TENSOR), P(DP, TENSOR), P(DP, TENSOR), P(TENSOR, None)),
        out_specs=(P(DP, TENSOR), P(DP, TENSOR), P(TENSOR, None)),
        check_vma=False,
    )
```

```python
import jax
import jax.numpy as jnp
from jax import lax
from jax.experimental import pallas as pl
from jax.experimental.pallas import tpu as pltpu
from jax.sharding import Mesh, PartitionSpec as P

BF = jnp.bfloat16
F32 = jnp.float32
HIGHEST = lax.Precision.HIGHEST
CHIPS = ("y", "x")
DP = ("y", "x", "core")
TENSOR = ("zl", "zh")
N_ZL = 4
N_CHIP = 32
REPLICAS = 64
D_IN = 3072
HALF = D_IN // 2
QUARTER = D_IN // 4
SLAB = D_IN // 8
PIECE = D_IN // REPLICAS
TOK = 256
COLS = 128
RANK = 32
EARLY = 32


def dot(a, b, dims, precision=None):
    return lax.dot_general(a, b, (dims, ((), ())), precision=precision, preferred_element_type=F32)


def tail_kernel(
    place_ref, mean_ref, own_ref, other_ref, warm_ref, near_ref, far_ref, weight_ref,
    fresh_ref, right_ref, input_grad_ref,
    own_buf, other_buf, fresh_buf, out_grad_buf, weight_buf, sems, out_sems,
):
    zh, zl = place_ref[0], place_ref[1]
    loads = [
        pltpu.make_async_copy(near_ref, out_grad_buf.at[0], sems.at[0]),
        pltpu.make_async_copy(far_ref, out_grad_buf.at[1], sems.at[1]),
        pltpu.make_async_copy(weight_ref, weight_buf, sems.at[2]),
        pltpu.make_async_copy(own_ref, own_buf, sems.at[3]),
        pltpu.make_async_copy(other_ref, other_buf, sems.at[4]),
    ]
    for load in loads:
        load.start()
    mean = mean_ref[...]
    warm = warm_ref[...]
    outer = dot(mean, mean, ((0,), (0,)))
    right = dot(warm, outer, ((1,), (0,)), HIGHEST)
    gram = dot(right, warm, ((1,), (1,)), HIGHEST)

    for load in loads[:3]:
        load.wait()
    total = jnp.zeros((TOK, SLAB), F32)
    for half in range(2):
        side = zh if half == 0 else 1 - zh
        for at in range(N_ZL):
            grads = out_grad_buf[side, at]
            block = (at * 2 + half) * 4
            rows = [weight_buf[core, block + x] for x in range(4) for core in range(2)]
            total += dot(grads, jnp.concatenate(rows, axis=0), ((1,), (1,)))
    input_grad_ref[...] = total.astype(BF)

    row_at = lax.broadcasted_iota(jnp.int32, (RANK, 1), 0)
    for k in range(RANK):
        scale = lax.rsqrt(gram[k : k + 1, k : k + 1])
        column = jnp.where(row_at > k, gram[:, k : k + 1] * scale, 0.0)
        own = row_at == k
        gram_row = gram[k : k + 1] * scale
        right_row = right[k : k + 1] * scale
        warm_row = warm[k : k + 1] * scale
        gram = jnp.where(own, gram_row, gram - column * gram_row)
        right = jnp.where(own, right_row, right - column * right_row)
        warm = jnp.where(own, warm_row, warm - column * warm_row)
    right_ref[...] = right
    mix = dot(warm, right, ((0,), (0,)), HIGHEST)
    high = mix.astype(BF)
    low = (mix - high.astype(F32)).astype(BF)

    for load in loads[3:]:
        load.wait()
    stores = []
    for core in range(2):
        for side in range(2):
            at = core * 2 + side
            block = mean_ref[at * QUARTER : (at + 1) * QUARTER, :]
            approx = dot(block, high, ((1,), (0,))) + dot(block, low, ((1,), (0,)))
            merged = (own_buf, other_buf)[side][core * QUARTER : (core + 1) * QUARTER]
            fresh_buf[at] = merged - approx
            half = zh if side == 0 else 1 - zh
            for slab in range(2):
                owner = (zl + N_ZL - (core * 2 + slab)) % N_ZL
                start = pl.multiple_of((owner * 2 + half) * SLAB, SLAB)
                store = pltpu.make_async_copy(
                    fresh_buf.at[at, pl.ds(slab * SLAB, SLAB)],
                    fresh_ref.at[pl.ds(start, SLAB)],
                    out_sems.at[at, slab],
                )
                store.start()
                stores.append(store)
    for store in stores:
        store.wait()


def tail_call(place, mean, own_merged, other_merged, warm, near, far, weights):
    in_vmem = pl.BlockSpec(memory_space=pltpu.VMEM)
    in_hbm = pl.BlockSpec(memory_space=pl.ANY)
    return pl.pallas_call(
        tail_kernel,
        in_specs=[pl.BlockSpec(memory_space=pltpu.SMEM), in_vmem, in_hbm, in_hbm, in_vmem] + [in_hbm] * 3,
        out_specs=[in_hbm, in_vmem, in_vmem],
        out_shape=[
            jax.ShapeDtypeStruct((D_IN, COLS), F32),
            jax.ShapeDtypeStruct((RANK, COLS), F32),
            jax.ShapeDtypeStruct((TOK, SLAB), BF),
        ],
        scratch_shapes=[
            pltpu.VMEM((HALF, COLS), F32),
            pltpu.VMEM((HALF, COLS), F32),
            pltpu.VMEM((4, QUARTER, COLS), F32),
            pltpu.VMEM((2, N_ZL, TOK, COLS), BF),
            pltpu.VMEM((2, N_CHIP, PIECE, COLS), BF),
            pltpu.SemaphoreType.DMA((5,)),
            pltpu.SemaphoreType.DMA((4, 2)),
        ],
        compiler_params=pltpu.CompilerParams(vmem_limit_bytes=32 * 1024 * 1024),
        cost_estimate=pl.CostEstimate(flops=8 * COLS * COLS * D_IN, bytes_accessed=5000000, transcendentals=32),
        name="basis_feedback_input_grad",
    )(place, mean, own_merged, other_merged, warm, near, far, weights)


def swap_halves(block):
    return lax.ppermute(block, "zh", [(0, 1), (1, 0)])


def pick(block, at):
    return lax.dynamic_index_in_dim(block, at, 0, keepdims=False)


def to_all_chips(block):
    spread = lax.optimization_barrier(jnp.broadcast_to(block[None], (N_CHIP,) + block.shape))
    return lax.all_to_all(spread, CHIPS, 0, 0)


def on_device(features, out_grad, weight, feedback, warm_basis):
    core = lax.axis_index("core")
    zh = lax.axis_index("zh")
    zl = lax.axis_index("zl")
    barrier = lax.optimization_barrier

    partner_out_grad = swap_halves(out_grad)
    plane = [(i * 8 + j, j * 8 + i) for i in range(8) for j in range(8)]
    turned = lax.ppermute(weight, ("y",) + TENSOR, plane)

    shifted = [features] + [
        lax.ppermute(features, "zl", [(i, (i + k) % N_ZL) for i in range(N_ZL)]) for k in range(1, N_ZL)
    ]
    spread = jnp.broadcast_to(turned[None, :EARLY], (N_CHIP, EARLY, COLS))
    shifted, spread = barrier((shifted, spread))
    gathered = jnp.concatenate(shifted, axis=1)
    sent = dot(gathered, partner_out_grad, ((0,), (0,))).astype(BF)
    other_grads = swap_halves(sent)
    early_weights = lax.all_to_all(spread, CHIPS, 0, 0)
    natural = feedback.reshape(N_ZL, 2, SLAB, COLS)
    slabs = [lax.dynamic_slice_in_dim(natural, (zl + N_ZL - k) % N_ZL, 1) for k in range(N_ZL)]
    slabs = barrier(jnp.concatenate(slabs, axis=0))

    def add_feedback(grads, half):
        own = lax.dynamic_slice(slabs, (0, half, 0, 0), (N_ZL, 1, SLAB, COLS))
        return (grads.reshape(own.shape).astype(F32) + own).reshape(HALF, COLS)

    own_merged = add_feedback(dot(gathered, out_grad, ((0,), (0,))), zh)

    other_merged = add_feedback(other_grads, 1 - zh)

    def quarters(at):
        return jnp.stack([pick(rows.reshape(2, QUARTER, COLS), at) for rows in (own_merged, other_merged)])

    swapped = lax.all_gather(quarters(1 - core).astype(BF), "core", axis=0)
    chips = (quarters(core) + pick(swapped, 1 - core).astype(F32)).astype(BF).reshape(N_CHIP, PIECE, COLS)

    late_weight = jnp.broadcast_to(turned[None, EARLY:], (N_CHIP, PIECE - EARLY, COLS))
    load = jnp.concatenate([chips, late_weight], axis=1)
    load, early_weights, late, late_grads = barrier((load, early_weights, out_grad, other_grads))
    arrived = lax.all_to_all(load, CHIPS, 0, 0)
    near = lax.all_gather(late, "zl", axis=0)
    arrived, near, late_grads = barrier((arrived, near, late_grads))
    parts = arrived[:, :PIECE]

    piece = (jnp.sum(parts.astype(F32), axis=0) / REPLICAS).astype(BF)
    piece, early_weights, arrived, near, late_grads = barrier((piece, early_weights, arrived, near, late_grads))
    chip_weights = jnp.concatenate([early_weights, arrived[:, PIECE:]], axis=1)
    far = swap_halves(near)
    late_merged = add_feedback(late_grads, 1 - zh)
    weights = lax.all_gather(chip_weights, "core", axis=0)
    all_means = lax.all_gather(to_all_chips(piece), "core", axis=0).reshape(D_IN, COLS)
    place = jnp.stack([zh, zl]).astype(jnp.int32)
    new_feedback, right, input_grad = tail_call(
        place, all_means, own_merged, late_merged, warm_basis.T, near, far, weights
    )
    return (input_grad, new_feedback, right.T)


def solution(mesh):
    grid = Mesh(mesh.devices.reshape(8, 4, 2, 4, 2), DP + TENSOR)
    return jax.shard_map(
        on_device,
        mesh=grid,
        in_specs=(P(DP, TENSOR), P(DP, TENSOR), P(DP, TENSOR), P(DP, TENSOR), P(TENSOR, None)),
        out_specs=(P(DP, TENSOR), P(DP, TENSOR), P(TENSOR, None)),
        check_vma=False,
    )
```

```python
import jax
import jax.numpy as jnp
from jax import lax
from jax.experimental import pallas as pl
from jax.experimental.pallas import tpu as pltpu
from jax.sharding import Mesh, PartitionSpec as P

BF = jnp.bfloat16
F32 = jnp.float32
HIGHEST = lax.Precision.HIGHEST
CHIPS = ("y", "x")
DP = ("y", "x", "core")
TENSOR = ("zl", "zh")
N_ZL = 4
N_CHIP = 32
REPLICAS = 64
D_IN = 3072
HALF = D_IN // 2
QUARTER = D_IN // 4
SLAB = D_IN // 8
PIECE = D_IN // REPLICAS
TOK = 256
COLS = 128
RANK = 32
EARLY = 24


def dot(a, b, dims, precision=None):
    return lax.dot_general(a, b, (dims, ((), ())), precision=precision, preferred_element_type=F32)


def tail_kernel(
    place_ref, mean_ref, own_ref, other_ref, warm_ref, near_ref, far_ref, weight_ref,
    fresh_ref, right_ref, input_grad_ref,
    own_buf, other_buf, fresh_buf, out_grad_buf, weight_buf, sems, out_sems,
):
    zh, zl = place_ref[0], place_ref[1]
    loads = [
        pltpu.make_async_copy(near_ref, out_grad_buf.at[0], sems.at[0]),
        pltpu.make_async_copy(far_ref, out_grad_buf.at[1], sems.at[1]),
        pltpu.make_async_copy(weight_ref, weight_buf, sems.at[2]),
        pltpu.make_async_copy(own_ref, own_buf, sems.at[3]),
        pltpu.make_async_copy(other_ref, other_buf, sems.at[4]),
    ]
    for load in loads:
        load.start()
    mean = mean_ref[...]
    warm = warm_ref[...]
    outer = dot(mean, mean, ((0,), (0,)))
    right = dot(warm, outer, ((1,), (0,)), HIGHEST)
    gram = dot(right, warm, ((1,), (1,)), HIGHEST)

    for load in loads[:3]:
        load.wait()
    total = jnp.zeros((TOK, SLAB), F32)
    for half in range(2):
        side = zh if half == 0 else 1 - zh
        for at in range(N_ZL):
            grads = out_grad_buf[side, at]
            block = (at * 2 + half) * 4
            rows = [weight_buf[core, block + x] for x in range(4) for core in range(2)]
            total += dot(grads, jnp.concatenate(rows, axis=0), ((1,), (1,)))
    input_grad_ref[...] = total.astype(BF)

    row_at = lax.broadcasted_iota(jnp.int32, (RANK, 1), 0)
    for k in range(RANK):
        scale = lax.rsqrt(gram[k : k + 1, k : k + 1])
        column = jnp.where(row_at > k, gram[:, k : k + 1] * scale, 0.0)
        own = row_at == k
        gram_row = gram[k : k + 1] * scale
        right_row = right[k : k + 1] * scale
        warm_row = warm[k : k + 1] * scale
        gram = jnp.where(own, gram_row, gram - column * gram_row)
        right = jnp.where(own, right_row, right - column * right_row)
        warm = jnp.where(own, warm_row, warm - column * warm_row)
    right_ref[...] = right
    mix = dot(warm, right, ((0,), (0,)), HIGHEST)
    high = mix.astype(BF)
    low = (mix - high.astype(F32)).astype(BF)

    for load in loads[3:]:
        load.wait()
    stores = []
    for core in range(2):
        for side in range(2):
            at = core * 2 + side
            block = mean_ref[at * QUARTER : (at + 1) * QUARTER, :]
            approx = dot(block, high, ((1,), (0,))) + dot(block, low, ((1,), (0,)))
            merged = (own_buf, other_buf)[side][core * QUARTER : (core + 1) * QUARTER]
            fresh_buf[at] = merged - approx
            half = zh if side == 0 else 1 - zh
            for slab in range(2):
                owner = (zl + N_ZL - (core * 2 + slab)) % N_ZL
                start = pl.multiple_of((owner * 2 + half) * SLAB, SLAB)
                store = pltpu.make_async_copy(
                    fresh_buf.at[at, pl.ds(slab * SLAB, SLAB)],
                    fresh_ref.at[pl.ds(start, SLAB)],
                    out_sems.at[at, slab],
                )
                store.start()
                stores.append(store)
    for store in stores:
        store.wait()


def tail_call(place, mean, own_merged, other_merged, warm, near, far, weights):
    in_vmem = pl.BlockSpec(memory_space=pltpu.VMEM)
    in_hbm = pl.BlockSpec(memory_space=pl.ANY)
    return pl.pallas_call(
        tail_kernel,
        in_specs=[pl.BlockSpec(memory_space=pltpu.SMEM), in_vmem, in_hbm, in_hbm, in_vmem] + [in_hbm] * 3,
        out_specs=[in_hbm, in_vmem, in_vmem],
        out_shape=[
            jax.ShapeDtypeStruct((D_IN, COLS), F32),
            jax.ShapeDtypeStruct((RANK, COLS), F32),
            jax.ShapeDtypeStruct((TOK, SLAB), BF),
        ],
        scratch_shapes=[
            pltpu.VMEM((HALF, COLS), F32),
            pltpu.VMEM((HALF, COLS), F32),
            pltpu.VMEM((4, QUARTER, COLS), F32),
            pltpu.VMEM((2, N_ZL, TOK, COLS), BF),
            pltpu.VMEM((2, N_CHIP, PIECE, COLS), BF),
            pltpu.SemaphoreType.DMA((5,)),
            pltpu.SemaphoreType.DMA((4, 2)),
        ],
        compiler_params=pltpu.CompilerParams(vmem_limit_bytes=32 * 1024 * 1024),
        cost_estimate=pl.CostEstimate(flops=8 * COLS * COLS * D_IN, bytes_accessed=5000000, transcendentals=32),
        name="basis_feedback_input_grad",
    )(place, mean, own_merged, other_merged, warm, near, far, weights)


def swap_halves(block):
    return lax.ppermute(block, "zh", [(0, 1), (1, 0)])


def pick(block, at):
    return lax.dynamic_index_in_dim(block, at, 0, keepdims=False)


def to_all_chips(block):
    spread = lax.optimization_barrier(jnp.broadcast_to(block[None], (N_CHIP,) + block.shape))
    return lax.all_to_all(spread, CHIPS, 0, 0)


def on_device(features, out_grad, weight, feedback, warm_basis):
    core = lax.axis_index("core")
    zh = lax.axis_index("zh")
    zl = lax.axis_index("zl")
    barrier = lax.optimization_barrier

    partner_out_grad = swap_halves(out_grad)
    plane = [(i * 8 + j, j * 8 + i) for i in range(8) for j in range(8)]
    turned = lax.ppermute(weight, ("y",) + TENSOR, plane)

    shifted = [features] + [
        lax.ppermute(features, "zl", [(i, (i + k) % N_ZL) for i in range(N_ZL)]) for k in range(1, N_ZL)
    ]
    spread = jnp.broadcast_to(turned[None, :EARLY], (N_CHIP, EARLY, COLS))
    shifted, spread = barrier((shifted, spread))
    gathered = jnp.concatenate(shifted, axis=1)
    sent = dot(gathered, partner_out_grad, ((0,), (0,))).astype(BF)
    other_grads = swap_halves(sent)
    early_weights = lax.all_to_all(spread, CHIPS, 0, 0)
    natural = feedback.reshape(N_ZL, 2, SLAB, COLS)
    slabs = [lax.dynamic_slice_in_dim(natural, (zl + N_ZL - k) % N_ZL, 1) for k in range(N_ZL)]
    slabs = barrier(jnp.concatenate(slabs, axis=0))

    def add_feedback(grads, half):
        own = lax.dynamic_slice(slabs, (0, half, 0, 0), (N_ZL, 1, SLAB, COLS))
        return (grads.reshape(own.shape).astype(F32) + own).reshape(HALF, COLS)

    own_merged = add_feedback(dot(gathered, out_grad, ((0,), (0,))), zh)

    other_merged = add_feedback(other_grads, 1 - zh)

    def quarters(at):
        return jnp.stack([pick(rows.reshape(2, QUARTER, COLS), at) for rows in (own_merged, other_merged)])

    swapped = lax.all_gather(quarters(1 - core).astype(BF), "core", axis=0)
    chips = (quarters(core) + pick(swapped, 1 - core).astype(F32)).astype(BF).reshape(N_CHIP, PIECE, COLS)

    late_weight = jnp.broadcast_to(turned[None, EARLY:], (N_CHIP, PIECE - EARLY, COLS))
    load = jnp.concatenate([chips, late_weight], axis=1)
    load, early_weights, late, late_grads = barrier((load, early_weights, out_grad, other_grads))
    arrived = lax.all_to_all(load, CHIPS, 0, 0)
    near = lax.all_gather(late, "zl", axis=0)
    arrived, near, late_grads = barrier((arrived, near, late_grads))
    parts = arrived[:, :PIECE]

    piece = (jnp.sum(parts.astype(F32), axis=0) / REPLICAS).astype(BF)
    piece, early_weights, arrived, near, late_grads = barrier((piece, early_weights, arrived, near, late_grads))
    chip_weights = jnp.concatenate([early_weights, arrived[:, PIECE:]], axis=1)
    far = swap_halves(near)
    late_merged = add_feedback(late_grads, 1 - zh)
    weights = lax.all_gather(chip_weights, "core", axis=0)
    all_means = lax.all_gather(to_all_chips(piece), "core", axis=0).reshape(D_IN, COLS)
    place = jnp.stack([zh, zl]).astype(jnp.int32)
    new_feedback, right, input_grad = tail_call(
        place, all_means, own_merged, late_merged, warm_basis.T, near, far, weights
    )
    return (input_grad, new_feedback, right.T)


def solution(mesh):
    grid = Mesh(mesh.devices.reshape(8, 4, 2, 4, 2), DP + TENSOR)
    return jax.shard_map(
        on_device,
        mesh=grid,
        in_specs=(P(DP, TENSOR), P(DP, TENSOR), P(DP, TENSOR), P(DP, TENSOR), P(TENSOR, None)),
        out_specs=(P(DP, TENSOR), P(DP, TENSOR), P(TENSOR, None)),
        check_vma=False,
    )
```
